32 devices in a mesh: parts: 2 (over y), leaf: 4 (over z), inner: 2 (over x), sub: 2 (over core).
Axes of the slice: x: 2, y: 2, z: 4, core: 2. Of those that a mesh axis runs over, the one named last changes fastest.
Arguments:
- points: bfloat16 [8192, 256], P(('parts', 'leaf', 'inner', 'sub')), parts along dimension 0, may hold values from -0.5 to 0.5
- exemplars: bfloat16 [8, 1024, 256], P(('parts', 'leaf')), parts along dimension 0, may hold values from -0.5 to 0.5
- selection: int32 [2, 8, 1024], P(None, ('parts', 'leaf')), parts along dimension 1, may hold values from 0 to 2047, as said below
Outputs:
- gains: float32 [2, 8, 2048], P(None, ('parts', 'leaf')), parts along dimension 1
- cover: float32 [8192], P(('parts', 'leaf', 'inner', 'sub')), parts along dimension 0
The draws below stay inside these ranges and needn't reach their ends.
There are 2 independent parts, one for each index of `parts`. The reference program is written for one: setup_inputs(seed, part) draws one part's arguments, and reference() takes and returns one part's arrays. A program takes and returns all parts, laid end to end along the dimension named above; each array names one. Nothing has to cross between parts.
Inputs may be any that keep to these rules, and one draw needn't show every extreme that they name: `selection`: each row holds distinct values; the rows of level l are equal for all groups g with the same g // 2 ** (l + 1).
All inputs are finite; a program needn't handle non-finite values.
Results may differ from the reference program's by a relative error of at most 0.0003.
Values may be sent and summed in bfloat16 or wider, within the bound.
A program may use at most 64 MiB of HBM per device.

```python
import jax
import jax.numpy as jnp
from jax import lax

DIM = 256
EX = 1024
GROUPS = 4
LEVELS = 2
POINTS = 4096


def draw_selection(key, part):
    key = jax.random.fold_in(key, 7)
    level_rows = []
    for height in range(LEVELS):
        span_size = 2 ** (height + 1)
        count = GROUPS // span_size
        keys = jax.random.split(jax.random.fold_in(key, height), count)
        picks = jax.vmap(lambda single: jax.random.permutation(single, 2 * EX)[:EX])(keys)
        level_rows.append(jnp.repeat(picks.astype(jnp.int32), span_size, axis=0))
    return jnp.stack(level_rows)


def block_scale(rng, extent, shards, least, high):
    loudness = 1.0
    for dim, shards_of in shards:
        steps = jax.random.uniform(jax.random.fold_in(jax.random.fold_in(rng, 6), dim), (shards_of,), jnp.float32, least / len(shards), high / len(shards))
        loudness = loudness * jnp.repeat(jnp.exp(steps), extent[dim] // shards_of).reshape((-1,) + (1,) * (len(extent) - 1 - dim))
    return loudness


def centred(stream_key, dims, scale, limit, cuts=(), kind=jnp.bfloat16):
    array = jax.random.normal(stream_key, dims, jnp.float32) * scale
    if len(cuts) > 0:
        array = block_scale(stream_key, dims, cuts, -0.22, 0.18) * array
    return jnp.clip(array, min=-limit, max=limit).astype(kind)


def setup_inputs(seed: int = 0, part: int = 0) -> dict:
    splits = jax.random.split(jax.random.key(seed), 4)
    own_keys = jax.random.split(jax.random.fold_in(splits[3], part), 4)
    points = centred(own_keys[0], (POINTS, DIM), 0.0625, 0.5, ((0, 16),))
    exemplars = centred(own_keys[1], (GROUPS, EX, DIM), 0.0625, 0.5, ((0, 4),))
    selection = draw_selection(jax.random.fold_in(jax.random.fold_in(splits[3], part), 71), part)
    return dict(points=points, exemplars=exemplars, selection=selection)


def reference(points, exemplars, selection):
    group_index = jnp.arange(GROUPS, dtype=jnp.int32)
    blocks = [exemplars]
    for height in range(LEVELS):
        span_bit = 2 ** height
        is_upper = (group_index // span_bit) % 2
        partner_index = group_index + span_bit - 2 * span_bit * is_upper
        current = blocks[-1]
        partner = current[partner_index]
        flag = (is_upper == 1)[:, None, None]
        merged = jnp.where(flag, jnp.concatenate([partner, current], 1), jnp.concatenate([current, partner], 1))
        chosen = jnp.take_along_axis(merged, selection[height][:, :, None], axis=1)
        blocks.append(chosen)
    stacked = jnp.stack(blocks[:LEVELS])
    leaf_points = points.reshape(GROUPS, -1, DIM)

    def one_group(packed):
        group_points, group_id = packed
        own_sims = jnp.dot(group_points, stacked[0, group_id].T, preferred_element_type=jnp.float32)
        gain_terms = []
        for height in range(LEVELS):
            span_bit = 2 ** height
            is_upper = (group_id // span_bit) % 2
            partner_id = group_id + span_bit - 2 * span_bit * is_upper
            partner_sims = jnp.dot(group_points, stacked[height, partner_id].T, preferred_element_type=jnp.float32)
            merged_sims = jnp.where(is_upper == 1, jnp.concatenate([partner_sims, own_sims], 1), jnp.concatenate([own_sims, partner_sims], 1))
            coverage = jnp.max(own_sims, 1)
            gain_terms.append(jnp.sum(jnp.maximum(merged_sims - coverage[:, None], jnp.float32(0.0)), 0))
            own_sims = jnp.take(merged_sims, selection[height, group_id], axis=1)
        final = jnp.max(own_sims, 1)
        return jnp.stack(gain_terms), final

    terms, cover = lax.map(one_group, (leaf_points, group_index))
    level_rows = []
    for height in range(LEVELS):
        span_size = 2 ** (height + 1)
        summed = terms[:, height].reshape(GROUPS // span_size, span_size, 2 * EX).sum(1)
        level_rows.append(jnp.repeat(summed, span_size, axis=0))
    return jnp.stack(level_rows), cover.reshape(-1)
```

```python
import functools

import jax
import jax.numpy as jnp
from jax import lax
from jax.experimental import pallas as pl
from jax.experimental.pallas import tpu as pltpu
from jax.sharding import PartitionSpec as P

MESH = pl.DeviceIdType.MESH
LANES = 128
CHUNK = 32
LOW = -1e30


def flipped(index, offset):
    out, bit = index, 1
    while bit <= offset:
        if offset & bit:
            out = out + bit * (1 - 2 * ((index // bit) % 2))
        bit *= 2
    return out


def as_row(tile):
    return jnp.concatenate([tile[k : k + 1] for k in range(tile.shape[0])], axis=1)


def as_tile(row):
    count = row.shape[1] // LANES
    return jnp.concatenate([row[:, k * LANES : (k + 1) * LANES] for k in range(count)], axis=0)


def marked(sel_tile, slots):
    sel = as_row(sel_tile)
    width = sel.shape[1]
    high, low = sel // LANES, sel % LANES
    tall = 2 * width // LANES
    high_hot = jnp.where(lax.broadcasted_iota(jnp.int32, (tall, width), 0) == high, 1.0, 0.0)
    if slots is not None:
        high_hot = high_hot * slots
    low_hot = jnp.where(lax.broadcasted_iota(jnp.int32, (LANES, width), 0) == low, 1.0, 0.0)
    return lax.dot_general(
        high_hot.astype(jnp.bfloat16),
        low_hot.astype(jnp.bfloat16),
        (((1,), (1,)), ((), ())),
        preferred_element_type=jnp.float32,
    )


def pick(table, index):
    high, low = index // LANES, index % LANES
    out = jnp.zeros(index.shape, table.dtype)
    for k in range(table.shape[0]):
        row = jnp.broadcast_to(table[k : k + 1], index.shape)
        value = jnp.take_along_axis(row, low, axis=1, mode="promise_in_bounds")
        out = jnp.where(high == k, value, out)
    return out


def kernel(
    levels, inner, sub,
    points, exemplars, selection, gains, cover,
    pts_in, sel_in, sims, bias, cov_out, cov_in, column, best, part_out, part_in, total_out, total_in,
    pts_send, pts_recv, sel_send, sel_recv, cov_send, cov_recv, part_send, part_recv, total_send, total_recv,
):
    span = 2**levels
    mates = inner * sub
    width = exemplars.shape[1]
    count = points.shape[0]
    tall = width // LANES
    my_leaf = lax.axis_index("leaf")
    bits = [(my_leaf // 2**height) % 2 for height in range(levels)]
    my_mate = lax.axis_index("inner") * sub + lax.axis_index("sub")

    leaf_ids = {d: {"leaf": flipped(my_leaf, d)} for d in range(1, span)}
    mate_ids = {}
    for k in range(1, mates):
        other = (my_mate + k) % mates
        mate_ids[k] = {"inner": other // sub, "sub": other % sub}

    barrier = pltpu.get_barrier_semaphore()
    for target in [*leaf_ids.values(), *mate_ids.values()]:
        pl.semaphore_signal(barrier, inc=1, device_id=target, device_id_type=MESH)
    pl.semaphore_wait(barrier, span - 1 + mates - 1)

    started = []

    def send(src, dst, send_sem, recv_sem, target):
        copy = pltpu.make_async_remote_copy(
            src_ref=src, dst_ref=dst, send_sem=send_sem, recv_sem=recv_sem,
            device_id=target, device_id_type=MESH,
        )
        copy.start()
        started.append(copy)
        return copy

    pts_copy, sel_copy, cov_copy, part_copy, total_copy = {}, {}, {}, {}, {}
    for d in range(1, span):
        pts_copy[d] = send(points, pts_in.at[d], pts_send.at[d], pts_recv.at[d], leaf_ids[d])
    for d in range(1, span):
        sel_copy[d] = send(selection, sel_in.at[d], sel_send.at[d], sel_recv.at[d], leaf_ids[d])

    def multiply(d):
        block = points if d == 0 else pts_in.at[d]
        sims[d] = lax.dot_general(
            block[...], exemplars[0], (((1,), (1,)), ((), ())), preferred_element_type=jnp.float32
        )

    def row_best(level, d):
        def body(i, carry):
            rows = pl.ds(pl.multiple_of(i * CHUNK, CHUNK), CHUNK)
            top = None
            for k in range(tall):
                lanes = pl.ds(k * LANES, LANES)
                value = sims[d, rows, lanes]
                if level > 0:
                    value = value + bias[level : level + 1, lanes]
                top = value if top is None else jnp.maximum(top, value)
            best[rows, :] = top
            return carry

        lax.fori_loop(0, count // CHUNK, body, 0)
        cov_out[level, d : d + 1] = jnp.max(best[...].T, axis=0, keepdims=True)

    def gain_sum(level, d, acc):
        row = None
        for s in range(span):
            if s >> level == d >> level:
                value = cov_out[level, d : d + 1] if s == 0 else cov_in[s, level, d ^ s : (d ^ s) + 1]
                row = value if row is None else jnp.maximum(row, value)
        column[...] = jnp.broadcast_to(row, (LANES, count)).T

        def body(i, total):
            rows = pl.ds(pl.multiple_of(i * CHUNK, CHUNK), CHUNK)
            base = column[rows, :]
            out = []
            for k in range(tall):
                value = jnp.maximum(sims[d, rows, k * LANES : (k + 1) * LANES] - base, 0.0)
                out.append(total[k] + value.reshape(CHUNK // 8, 8, LANES).sum(0))
            return tuple(out)

        return lax.fori_loop(0, count // CHUNK, body, acc)

    def finish(level, acc):
        part_out[level] = jnp.concatenate([jnp.sum(a, axis=0, keepdims=True) for a in acc], axis=0)

    def send_cov(level):
        for d in range(1, min(2 ** (level + 1), span)):
            cov_copy[level, d] = send(
                cov_out.at[level], cov_in.at[d, level], cov_send.at[level, d], cov_recv.at[level, d], leaf_ids[d]
            )

    none = tuple(jnp.zeros((8, LANES), jnp.float32) for _ in range(tall))

    multiply(0)
    row_best(0, 0)
    send_cov(0)
    for level in range(1, levels + 1):
        slots = None
        for height in reversed(range(level)):
            hits = marked(selection[height], slots)
            slots = as_row(jnp.where(bits[height] == 1, hits[tall:], hits[:tall]))
        bias[level : level + 1] = jnp.where(slots > 0.5, 0.0, LOW)

    for level in range(1, levels + 1):
        reach = 2**level
        last = level == levels
        if not last:
            for d in range(reach // 2, reach):
                pts_copy[d].wait_recv()
                multiply(d)
            for d in range(reach):
                row_best(level, d)
            send_cov(level)
        for d in range(1, reach):
            cov_copy[level - 1, d].wait_recv()
        acc = none
        for d in range(reach):
            if last and d >= reach // 2:
                pts_copy[d].wait_recv()
                multiply(d)
            acc = gain_sum(level - 1, d, acc)
        finish(level - 1, acc)

    for k in range(1, mates):
        part_copy[k] = send(part_out, part_in.at[k], part_send.at[k], part_recv.at[k], mate_ids[k])
    for d in range(span):
        row_best(levels, d)
    send_cov(levels)

    total = part_out[...]
    for k in range(1, mates):
        part_copy[k].wait_recv()
        total = total + part_in[k]
    total_out[...] = total
    for d in range(1, span):
        total_copy[d] = send(total_out, total_in.at[d], total_send.at[d], total_recv.at[d], leaf_ids[d])

    top = cov_out[levels, 0:1]
    for d in range(1, span):
        cov_copy[levels, d].wait_recv()
        top = jnp.maximum(top, cov_in[d, levels, d : d + 1])
    cover[...] = as_tile(top)

    for d in range(1, span):
        sel_copy[d].wait_recv()
        total_copy[d].wait_recv()
    for level in range(levels):
        blocks = [total_out[level] if d == 0 else total_in[d, level] for d in range(2 ** (level + 1))]
        for height in range(level + 1):
            step = 2**height
            for d in range(0, len(blocks), 2 * step):
                upper = bits[height] == 1
                mine, theirs = blocks[d], blocks[d + step]
                merged = jnp.concatenate(
                    [jnp.where(upper, theirs, mine), jnp.where(upper, mine, theirs)], axis=0
                )
                if height == level:
                    gains[level] = merged
                else:
                    blocks[d] = pick(merged, selection[height] if d == 0 else sel_in[d, height])
    for copy in started:
        copy.wait_send()


def on_device(points, exemplars, selection):
    levels = selection.shape[0]
    span = 2**levels
    inner, sub = lax.axis_size("inner"), lax.axis_size("sub")
    mates = inner * sub
    count, dim = points.shape
    width = exemplars.shape[1]
    tall = width // LANES
    cov_rows = max(8, span)
    f32 = jnp.float32
    dma = pltpu.SemaphoreType.DMA
    vmem = pl.BlockSpec(memory_space=pltpu.VMEM)
    gains, cover = pl.pallas_call(
        functools.partial(kernel, levels, inner, sub),
        out_shape=(
            jax.ShapeDtypeStruct((levels, 2 * tall, LANES), f32),
            jax.ShapeDtypeStruct((count // LANES, LANES), f32),
        ),
        in_specs=[vmem] * 3,
        out_specs=(vmem, vmem),
        scratch_shapes=[
            pltpu.VMEM((span, count, dim), points.dtype),
            pltpu.VMEM((span, levels, tall, LANES), jnp.int32),
            pltpu.VMEM((span, count, width), f32),
            pltpu.VMEM((max(8, levels + 1), width), f32),
            pltpu.VMEM((levels + 1, cov_rows, count), f32),
            pltpu.VMEM((span, levels + 1, cov_rows, count), f32),
            pltpu.VMEM((count, LANES), f32),
            pltpu.VMEM((count, LANES), f32),
            pltpu.VMEM((levels, tall, LANES), f32),
            pltpu.VMEM((mates, levels, tall, LANES), f32),
            pltpu.VMEM((levels, tall, LANES), f32),
            pltpu.VMEM((span, levels, tall, LANES), f32),
            dma((span,)), dma((span,)),
            dma((span,)), dma((span,)),
            dma((levels + 1, span)), dma((levels + 1, span)),
            dma((mates,)), dma((mates,)),
            dma((span,)), dma((span,)),
        ],
        compiler_params=pltpu.CompilerParams(
            collective_id=0, has_side_effects=True, vmem_limit_bytes=48 * 1024 * 1024
        ),
    )(points, exemplars, selection.reshape(levels, tall, LANES))
    return gains.reshape(levels, 1, 2 * width), cover.reshape(count)


def solution(mesh):
    placed = (
        P(("parts", "leaf", "inner", "sub"), None),
        P(("parts", "leaf"), None, None),
        P(None, ("parts", "leaf"), None),
    )
    return jax.shard_map(
        on_device,
        mesh=mesh,
        in_specs=placed,
        out_specs=(P(None, ("parts", "leaf"), None), P(("parts", "leaf", "inner", "sub"))),
        check_vma=False,
    )
```

```python
import functools

import jax
import jax.numpy as jnp
from jax import lax
from jax.experimental import pallas as pl
from jax.experimental.pallas import tpu as pltpu
from jax.sharding import PartitionSpec as P

MESH = pl.DeviceIdType.MESH
LANES = 128
CHUNK = 32
PARTS = 4
LOW = -1e30


def flipped(index, offset):
    out, bit = index, 1
    while bit <= offset:
        if offset & bit:
            out = out + bit * (1 - 2 * ((index // bit) % 2))
        bit *= 2
    return out


def as_row(tile):
    return jnp.concatenate([tile[k : k + 1] for k in range(tile.shape[0])], axis=1)


def as_tile(row):
    count = row.shape[1] // LANES
    return jnp.concatenate([row[:, k * LANES : (k + 1) * LANES] for k in range(count)], axis=0)


def marked(sel_tile, slots):
    sel = as_row(sel_tile)
    width = sel.shape[1]
    high, low = sel // LANES, sel % LANES
    tall = 2 * width // LANES
    high_hot = jnp.where(lax.broadcasted_iota(jnp.int32, (tall, width), 0) == high, 1.0, 0.0)
    if slots is not None:
        high_hot = high_hot * slots
    low_hot = jnp.where(lax.broadcasted_iota(jnp.int32, (LANES, width), 0) == low, 1.0, 0.0)
    return lax.dot_general(
        high_hot.astype(jnp.bfloat16),
        low_hot.astype(jnp.bfloat16),
        (((1,), (1,)), ((), ())),
        preferred_element_type=jnp.float32,
    )


def pick(table, index):
    high, low = index // LANES, index % LANES
    out = jnp.zeros(index.shape, table.dtype)
    for k in range(table.shape[0]):
        row = jnp.broadcast_to(table[k : k + 1], index.shape)
        value = jnp.take_along_axis(row, low, axis=1, mode="promise_in_bounds")
        out = jnp.where(high == k, value, out)
    return out


def kernel(
    levels, inner, sub,
    points, exemplars, selection, gains, cover,
    pts_in, ex_in, sel_own, sel_in, sims, bias, cov_out, cov_in, last_out, last_in, column, best,
    part_out, part_in, total_out, total_in,
    fetch_sem, pts_send, pts_recv, sel_send, sel_recv, cov_send, cov_recv, last_send, last_recv, part_send, part_recv, total_send, total_recv,
):
    span = 2**levels
    mates = inner * sub
    width = exemplars.shape[1]
    count = points.shape[0]
    tall = width // LANES
    my_leaf = lax.axis_index("leaf")
    bits = [(my_leaf // 2**height) % 2 for height in range(levels)]
    my_mate = lax.axis_index("inner") * sub + lax.axis_index("sub")

    leaf_ids = {d: {"leaf": flipped(my_leaf, d)} for d in range(1, span)}
    mate_ids = {}
    for k in range(1, mates):
        other = (my_mate + k) % mates
        mate_ids[k] = {"inner": other // sub, "sub": other % sub}

    here = my_leaf % span

    def block_of(d):
        return flipped(here, d)

    barrier = pltpu.get_barrier_semaphore()
    for target in [*leaf_ids.values(), *mate_ids.values()]:
        pl.semaphore_signal(barrier, inc=1, device_id=target, device_id_type=MESH)
    fetches = [
        pltpu.make_async_copy(points, pts_in.at[here], fetch_sem.at[0]),
        pltpu.make_async_copy(exemplars.at[0], ex_in, fetch_sem.at[1]),
        pltpu.make_async_copy(selection, sel_own, fetch_sem.at[2]),
    ]
    for fetch in fetches:
        fetch.start()

    started = []

    def send(src, dst, send_sem, recv_sem, target):
        copy = pltpu.make_async_remote_copy(
            src_ref=src, dst_ref=dst, send_sem=send_sem, recv_sem=recv_sem,
            device_id=target, device_id_type=MESH,
        )
        copy.start()
        started.append(copy)
        return copy

    sel_copy, cov_copy, last_copy, part_copy, total_copy = {}, {}, {}, {}, {}

    def passing(slot, part, side):
        rows = pl.ds(part * (count // PARTS), count // PARTS)
        return pltpu.make_async_remote_copy(
            src_ref=pts_in.at[slot, rows], dst_ref=pts_in.at[slot, rows],
            send_sem=pts_send.at[side, slot, part], recv_sem=pts_recv.at[slot, part],
            device_id={"leaf": my_leaf + 2 * side - 1}, device_id_type=MESH,
        )

    has_side = [here > 0, here < span - 1]

    def relay(distance, act):
        for part in range(PARTS):
            for side in (1, 0):
                slot = here - distance if side == 1 else here + distance
                inside = slot >= 0 if side == 1 else slot < span

                @pl.when(inside)
                def _():
                    copy = passing(slot, part, side)
                    act(copy, side)

    def arrive_and_pass(copy, side):
        copy.wait_recv()

        @pl.when(has_side[side])
        def _():
            copy.start()

    def start_own(copy, side):
        @pl.when(has_side[side])
        def _():
            copy.start()

    def finish_pass(copy, side):
        @pl.when(has_side[side])
        def _():
            copy.wait_send()

    def multiply(d):
        sims[d] = lax.dot_general(
            pts_in[block_of(d)], ex_in[...], (((1,), (1,)), ((), ())), preferred_element_type=jnp.float32
        )

    def row_best(level, d):
        def body(i, carry):
            rows = pl.ds(pl.multiple_of(i * CHUNK, CHUNK), CHUNK)
            top = None
            for k in range(tall):
                lanes = pl.ds(k * LANES, LANES)
                value = sims[d, rows, lanes]
                if level > 0:
                    value = value + bias[level : level + 1, lanes]
                top = value if top is None else jnp.maximum(top, value)
            best[rows, :] = top
            return carry

        lax.fori_loop(0, count // CHUNK, body, 0)
        row = jnp.max(best[...].T, axis=0, keepdims=True)
        if level == levels:
            last_out[d] = as_tile(row)
            if d > 0:
                last_copy[d] = send(
                    last_out.at[d], last_in.at[d], last_send.at[d], last_recv.at[d], leaf_ids[d]
                )
        else:
            cov_out[level, d : d + 1] = row

    def gain_sum(level, d, acc):
        row = None
        for s in range(span):
            if s >> level == d >> level:
                value = cov_out[level, d : d + 1] if s == 0 else cov_in[s, level, d ^ s : (d ^ s) + 1]
                row = value if row is None else jnp.maximum(row, value)
        column[...] = jnp.broadcast_to(row, (LANES, count)).T

        def body(i, total):
            rows = pl.ds(pl.multiple_of(i * CHUNK, CHUNK), CHUNK)
            base = column[rows, :]
            out = []
            for k in range(tall):
                value = jnp.maximum(sims[d, rows, k * LANES : (k + 1) * LANES] - base, 0.0)
                out.append(total[k] + value.reshape(CHUNK // 8, 8, LANES).sum(0))
            return tuple(out)

        return lax.fori_loop(0, count // CHUNK, body, acc)

    def finish(level, acc):
        part_out[level] = jnp.concatenate([jnp.sum(a, axis=0, keepdims=True) for a in acc], axis=0)

    def send_cov(level):
        for d in range(1, min(2 ** (level + 1), span)):
            cov_copy[level, d] = send(
                cov_out.at[level], cov_in.at[d, level], cov_send.at[level, d], cov_recv.at[level, d], leaf_ids[d]
            )

    none = tuple(jnp.zeros((8, LANES), jnp.float32) for _ in range(tall))

    fetches[0].wait()
    fetches[1].wait()
    multiply(0)
    row_best(0, 0)
    pl.semaphore_wait(barrier, span - 1 + mates - 1)
    relay(0, start_own)
    send_cov(0)
    fetches[2].wait()
    for level in range(1, levels + 1):
        slots = None
        for height in reversed(range(level)):
            hits = marked(sel_own[height], slots)
            slots = as_row(jnp.where(bits[height] == 1, hits[tall:], hits[:tall]))
        bias[level : level + 1] = jnp.where(slots > 0.5, 0.0, LOW)

    level, acc = 1, none
    for d in range(1, span):
        relay(d, arrive_and_pass)
        if d == 2 ** (level - 1) :
            for e in range(1, d + d):
                cov_copy[level - 1, e].wait_recv()
            acc = none
            for e in range(d):
                acc = gain_sum(level - 1, e, acc)
        multiply(d)
        acc = gain_sum(level - 1, d, acc)
        if d == 2**level - 1:
            finish(level - 1, acc)
            if level < levels:
                for e in range(d + 1):
                    row_best(level, e)
                send_cov(level)
                if level == levels - 1:
                    for e in range(d + 1):
                        row_best(levels, e)
            level += 1

    for k in range(1, mates):
        part_copy[k] = send(part_out, part_in.at[k], part_send.at[k], part_recv.at[k], mate_ids[k])
    for d in range(2, span, 2):
        sel_copy[d] = send(sel_own, sel_in.at[d], sel_send.at[d], sel_recv.at[d], leaf_ids[d])
    for d in range(span // 2 if levels > 1 else 0, span):
        row_best(levels, d)

    total = part_out[...]
    for k in range(1, mates):
        part_copy[k].wait_recv()
        total = total + part_in[k]
    total_out[...] = total
    for d in range(1, span):
        total_copy[d] = send(total_out, total_in.at[d], total_send.at[d], total_recv.at[d], leaf_ids[d])

    top = last_out[0]
    for d in range(1, span):
        last_copy[d].wait_recv()
        top = jnp.maximum(top, last_in[d])
    cover[...] = top

    for d in range(1, span):
        total_copy[d].wait_recv()
    for copy in sel_copy.values():
        copy.wait_recv()
    for level in range(levels):
        blocks = [total_out[level] if d == 0 else total_in[d, level] for d in range(2 ** (level + 1))]
        for height in range(level + 1):
            step = 2**height
            for d in range(0, len(blocks), 2 * step):
                upper = bits[height] == 1
                mine, theirs = blocks[d], blocks[d + step]
                merged = jnp.concatenate(
                    [jnp.where(upper, theirs, mine), jnp.where(upper, mine, theirs)], axis=0
                )
                if height == level:
                    gains[level] = merged
                else:
                    blocks[d] = pick(merged, sel_own[height] if d == 0 else sel_in[d, height])
    for copy in started:
        copy.wait_send()
    for distance in range(span - 1):
        relay(distance, finish_pass)


def hand_out(gains_in, cover_in, gains, cover):
    gains[...] = gains_in[...]
    cover[...] = cover_in[...]


def on_device(points, exemplars, selection):
    levels = selection.shape[0]
    span = 2**levels
    inner, sub = lax.axis_size("inner"), lax.axis_size("sub")
    mates = inner * sub
    count, dim = points.shape
    width = exemplars.shape[1]
    tall = width // LANES
    cov_rows = max(8, span)
    f32 = jnp.float32
    dma = pltpu.SemaphoreType.DMA
    vmem = pl.BlockSpec(memory_space=pltpu.VMEM)
    gains, cover = pl.pallas_call(
        functools.partial(kernel, levels, inner, sub),
        out_shape=(
            jax.ShapeDtypeStruct((levels, 2 * tall, LANES), f32),
            jax.ShapeDtypeStruct((count // LANES, LANES), f32),
        ),
        in_specs=[pl.BlockSpec(memory_space=pltpu.HBM)] * 3,
        out_specs=(vmem, vmem),
        scratch_shapes=[
            pltpu.VMEM((span, count, dim), points.dtype),
            pltpu.VMEM((width, dim), exemplars.dtype),
            pltpu.VMEM((levels, tall, LANES), jnp.int32),
            pltpu.VMEM((span, levels, tall, LANES), jnp.int32),
            pltpu.VMEM((span, count, width), f32),
            pltpu.VMEM((max(8, levels + 1), width), f32),
            pltpu.VMEM((levels, cov_rows, count), f32),
            pltpu.VMEM((span, levels, cov_rows, count), f32),
            pltpu.VMEM((span, count // LANES, LANES), f32),
            pltpu.VMEM((span, count // LANES, LANES), f32),
            pltpu.VMEM((count, LANES), f32),
            pltpu.VMEM((count, LANES), f32),
            pltpu.VMEM((levels, tall, LANES), f32),
            pltpu.VMEM((mates, levels, tall, LANES), f32),
            pltpu.VMEM((levels, tall, LANES), f32),
            pltpu.VMEM((span, levels, tall, LANES), f32),
            dma((3,)),
            dma((2, span, PARTS)), dma((span, PARTS)),
            dma((span,)), dma((span,)),
            dma((levels, span)), dma((levels, span)),
            dma((span,)), dma((span,)),
            dma((mates,)), dma((mates,)),
            dma((span,)), dma((span,)),
        ],
        compiler_params=pltpu.CompilerParams(
            collective_id=0, has_side_effects=True, vmem_limit_bytes=64 * 1024 * 1024 - 65536
        ),
    )(points, exemplars, selection.reshape(levels, tall, LANES))
    gains, cover = pl.pallas_call(
        hand_out,
        out_shape=tuple(jax.ShapeDtypeStruct(x.shape, x.dtype) for x in (gains, cover)),
        in_specs=[vmem] * 2,
        out_specs=(vmem, vmem),
    )(gains, cover)
    return gains.reshape(levels, 1, 2 * width), cover.reshape(count)


def solution(mesh):
    placed = (
        P(("parts", "leaf", "inner", "sub"), None),
        P(("parts", "leaf"), None, None),
        P(None, ("parts", "leaf"), None),
    )
    return jax.shard_map(
        on_device,
        mesh=mesh,
        in_specs=placed,
        out_specs=(P(None, ("parts", "leaf"), None), P(("parts", "leaf", "inner", "sub"))),
        check_vma=False,
    )
```

```python
import functools

import jax
import jax.numpy as jnp
from jax import lax
from jax.experimental import pallas as pl
from jax.experimental.pallas import tpu as pltpu
from jax.sharding import PartitionSpec as P

MESH = pl.DeviceIdType.MESH
LANES = 128
CHUNK = 32
PARTS = 4
LOW = -1e30


def flipped(index, offset):
    out, bit = index, 1
    while bit <= offset:
        if offset & bit:
            out = out + bit * (1 - 2 * ((index // bit) % 2))
        bit *= 2
    return out


def as_row(tile):
    return jnp.concatenate([tile[k : k + 1] for k in range(tile.shape[0])], axis=1)


def as_tile(row):
    count = row.shape[1] // LANES
    return jnp.concatenate([row[:, k * LANES : (k + 1) * LANES] for k in range(count)], axis=0)


def marked(sel_tile, slots):
    sel = as_row(sel_tile)
    width = sel.shape[1]
    high, low = sel // LANES, sel % LANES
    tall = 2 * width // LANES
    high_hot = jnp.where(lax.broadcasted_iota(jnp.int32, (tall, width), 0) == high, 1.0, 0.0)
    if slots is not None:
        high_hot = high_hot * slots
    low_hot = jnp.where(lax.broadcasted_iota(jnp.int32, (LANES, width), 0) == low, 1.0, 0.0)
    return lax.dot_general(
        high_hot.astype(jnp.bfloat16),
        low_hot.astype(jnp.bfloat16),
        (((1,), (1,)), ((), ())),
        preferred_element_type=jnp.float32,
    )


def pick(table, index):
    high, low = index // LANES, index % LANES
    out = jnp.zeros(index.shape, table.dtype)
    for k in range(table.shape[0]):
        row = jnp.broadcast_to(table[k : k + 1], index.shape)
        value = jnp.take_along_axis(row, low, axis=1, mode="promise_in_bounds")
        out = jnp.where(high == k, value, out)
    return out


def kernel(
    levels, inner, sub,
    points, exemplars, selection, gains, cover,
    pts_in, ex_in, sel_own, sel_in, sims, bias, cov_out, cov_in, last_out, last_in, column, best,
    part_out, part_in, totals,
    fetch_sem, pts_send, pts_recv, sel_send, sel_recv, cov_send, cov_recv, last_send, last_recv, part_send, part_recv,
):
    span = 2**levels
    mates = inner * sub
    width = exemplars.shape[1]
    count = points.shape[0]
    tall = width // LANES
    my_leaf = lax.axis_index("leaf")
    bits = [(my_leaf // 2**height) % 2 for height in range(levels)]
    my_mate = lax.axis_index("inner") * sub + lax.axis_index("sub")

    leaf_ids = {d: {"leaf": flipped(my_leaf, d)} for d in range(1, span)}
    mate_ids = {}
    for k in range(1, mates):
        other = (my_mate + k) % mates
        mate_ids[k] = {"inner": other // sub, "sub": other % sub}

    here = my_leaf % span

    def block_of(d):
        return flipped(here, d)

    barrier = pltpu.get_barrier_semaphore()
    all_ids = {}
    for d in range(span):
        for k in range(mates):
            if d + k > 0:
                all_ids[d, k] = {**leaf_ids.get(d, {}), **mate_ids.get(k, {})}
    for target in all_ids.values():
        pl.semaphore_signal(barrier, inc=1, device_id=target, device_id_type=MESH)
    fetches = [
        pltpu.make_async_copy(points, pts_in.at[here], fetch_sem.at[0]),
        pltpu.make_async_copy(exemplars.at[0], ex_in, fetch_sem.at[1]),
        pltpu.make_async_copy(selection, sel_own, fetch_sem.at[2]),
    ]
    for fetch in fetches:
        fetch.start()

    started = []

    def send(src, dst, send_sem, recv_sem, target):
        copy = pltpu.make_async_remote_copy(
            src_ref=src, dst_ref=dst, send_sem=send_sem, recv_sem=recv_sem,
            device_id=target, device_id_type=MESH,
        )
        copy.start()
        started.append(copy)
        return copy

    sel_copy, cov_copy, last_copy, part_copy = {}, {}, {}, {}

    def passing(slot, part, side):
        rows = pl.ds(part * (count // PARTS), count // PARTS)
        return pltpu.make_async_remote_copy(
            src_ref=pts_in.at[slot, rows], dst_ref=pts_in.at[slot, rows],
            send_sem=pts_send.at[side, slot, part], recv_sem=pts_recv.at[slot, part],
            device_id={"leaf": my_leaf + 2 * side - 1}, device_id_type=MESH,
        )

    has_side = [here > 0, here < span - 1]

    def relay(distance, act):
        for part in range(PARTS):
            for side in (1, 0):
                slot = here - distance if side == 1 else here + distance
                inside = slot >= 0 if side == 1 else slot < span

                @pl.when(inside)
                def _():
                    copy = passing(slot, part, side)
                    act(copy, side)

    def arrive_and_pass(copy, side):
        copy.wait_recv()

        @pl.when(has_side[side])
        def _():
            copy.start()

    def start_own(copy, side):
        @pl.when(has_side[side])
        def _():
            copy.start()

    def finish_pass(copy, side):
        @pl.when(has_side[side])
        def _():
            copy.wait_send()

    def multiply(d):
        sims[d] = lax.dot_general(
            pts_in[block_of(d)], ex_in[...], (((1,), (1,)), ((), ())), preferred_element_type=jnp.float32
        )

    def row_best(level, d):
        def body(i, carry):
            rows = pl.ds(pl.multiple_of(i * CHUNK, CHUNK), CHUNK)
            top = None
            for k in range(tall):
                lanes = pl.ds(k * LANES, LANES)
                value = sims[d, rows, lanes]
                if level > 0:
                    value = value + bias[level : level + 1, lanes]
                top = value if top is None else jnp.maximum(top, value)
            best[rows, :] = top
            return carry

        lax.fori_loop(0, count // CHUNK, body, 0)
        row = jnp.max(best[...].T, axis=0, keepdims=True)
        if level == levels:
            last_out[d] = as_tile(row)
            if d > 0:
                last_copy[d] = send(
                    last_out.at[d], last_in.at[d], last_send.at[d], last_recv.at[d], leaf_ids[d]
                )
        else:
            cov_out[level, d : d + 1] = row

    def gain_sum(level, d, acc):
        row = None
        for s in range(span):
            if s >> level == d >> level:
                value = cov_out[level, d : d + 1] if s == 0 else cov_in[s, level, d ^ s : (d ^ s) + 1]
                row = value if row is None else jnp.maximum(row, value)
        column[...] = jnp.broadcast_to(row, (LANES, count)).T

        def body(i, total):
            rows = pl.ds(pl.multiple_of(i * CHUNK, CHUNK), CHUNK)
            base = column[rows, :]
            out = []
            for k in range(tall):
                value = jnp.maximum(sims[d, rows, k * LANES : (k + 1) * LANES] - base, 0.0)
                out.append(total[k] + value.reshape(CHUNK // 8, 8, LANES).sum(0))
            return tuple(out)

        return lax.fori_loop(0, count // CHUNK, body, acc)

    def finish(level, acc):
        part_out[level] = jnp.concatenate([jnp.sum(a, axis=0, keepdims=True) for a in acc], axis=0)

    def send_cov(level):
        for d in range(1, min(2 ** (level + 1), span)):
            cov_copy[level, d] = send(
                cov_out.at[level], cov_in.at[d, level], cov_send.at[level, d], cov_recv.at[level, d], leaf_ids[d]
            )

    none = tuple(jnp.zeros((8, LANES), jnp.float32) for _ in range(tall))

    fetches[0].wait()
    fetches[1].wait()
    multiply(0)
    row_best(0, 0)
    pl.semaphore_wait(barrier, span * mates - 1)
    relay(0, start_own)
    send_cov(0)
    fetches[2].wait()
    for level in range(1, levels + 1):
        slots = None
        for height in reversed(range(level)):
            hits = marked(sel_own[height], slots)
            slots = as_row(jnp.where(bits[height] == 1, hits[tall:], hits[:tall]))
        bias[level : level + 1] = jnp.where(slots > 0.5, 0.0, LOW)

    level, acc = 1, none
    for d in range(1, span):
        relay(d, arrive_and_pass)
        if d == 2 ** (level - 1) :
            for e in range(1, d + d):
                cov_copy[level - 1, e].wait_recv()
            acc = none
            for e in range(d):
                acc = gain_sum(level - 1, e, acc)
        multiply(d)
        acc = gain_sum(level - 1, d, acc)
        if d == 2**level - 1:
            finish(level - 1, acc)
            if level < levels:
                for e in range(d + 1):
                    row_best(level, e)
                send_cov(level)
                if level == levels - 1:
                    for e in range(d + 1):
                        row_best(levels, e)
            level += 1

    for d in reversed(range(span)):
        for k in range(mates):
            if d + k > 0:
                part_copy[d, k] = send(
                    part_out, part_in.at[d, k], part_send.at[d, k], part_recv.at[d, k], all_ids[d, k]
                )
    for d in range(2, span, 2):
        sel_copy[d] = send(sel_own, sel_in.at[d], sel_send.at[d], sel_recv.at[d], leaf_ids[d])
    for d in range(span // 2 if levels > 1 else 0, span):
        row_best(levels, d)

    top = last_out[0]
    for d in range(1, span):
        last_copy[d].wait_recv()
        top = jnp.maximum(top, last_in[d])
    cover[...] = top

    for d in range(span):
        total = part_out[...] if d == 0 else None
        for k in range(mates):
            if d + k > 0:
                part_copy[d, k].wait_recv()
                total = part_in[d, k] if total is None else total + part_in[d, k]
        totals[d] = total
    for copy in sel_copy.values():
        copy.wait_recv()
    for level in range(levels):
        blocks = [totals[d, level] for d in range(2 ** (level + 1))]
        for height in range(level + 1):
            step = 2**height
            for d in range(0, len(blocks), 2 * step):
                upper = bits[height] == 1
                mine, theirs = blocks[d], blocks[d + step]
                merged = jnp.concatenate(
                    [jnp.where(upper, theirs, mine), jnp.where(upper, mine, theirs)], axis=0
                )
                if height == level:
                    gains[level] = merged
                else:
                    blocks[d] = pick(merged, sel_own[height] if d == 0 else sel_in[d, height])
    for copy in started:
        copy.wait_send()
    for distance in range(span - 1):
        relay(distance, finish_pass)


def hand_out(gains_in, cover_in, gains, cover):
    gains[...] = gains_in[...]
    cover[...] = cover_in[...]


def on_device(points, exemplars, selection):
    levels = selection.shape[0]
    span = 2**levels
    inner, sub = lax.axis_size("inner"), lax.axis_size("sub")
    mates = inner * sub
    count, dim = points.shape
    width = exemplars.shape[1]
    tall = width // LANES
    cov_rows = max(8, span)
    f32 = jnp.float32
    dma = pltpu.SemaphoreType.DMA
    vmem = pl.BlockSpec(memory_space=pltpu.VMEM)
    gains, cover = pl.pallas_call(
        functools.partial(kernel, levels, inner, sub),
        out_shape=(
            jax.ShapeDtypeStruct((levels, 2 * tall, LANES), f32),
            jax.ShapeDtypeStruct((count // LANES, LANES), f32),
        ),
        in_specs=[pl.BlockSpec(memory_space=pltpu.HBM)] * 3,
        out_specs=(vmem, vmem),
        scratch_shapes=[
            pltpu.VMEM((span, count, dim), points.dtype),
            pltpu.VMEM((width, dim), exemplars.dtype),
            pltpu.VMEM((levels, tall, LANES), jnp.int32),
            pltpu.VMEM((span, levels, tall, LANES), jnp.int32),
            pltpu.VMEM((span, count, width), f32),
            pltpu.VMEM((max(8, levels + 1), width), f32),
            pltpu.VMEM((levels, cov_rows, count), f32),
            pltpu.VMEM((span, levels, cov_rows, count), f32),
            pltpu.VMEM((span, count // LANES, LANES), f32),
            pltpu.VMEM((span, count // LANES, LANES), f32),
            pltpu.VMEM((count, LANES), f32),
            pltpu.VMEM((count, LANES), f32),
            pltpu.VMEM((levels, tall, LANES), f32),
            pltpu.VMEM((span, mates, levels, tall, LANES), f32),
            pltpu.VMEM((span, levels, tall, LANES), f32),
            dma((3,)),
            dma((2, span, PARTS)), dma((span, PARTS)),
            dma((span,)), dma((span,)),
            dma((levels, span)), dma((levels, span)),
            dma((span,)), dma((span,)),
            dma((span, mates)), dma((span, mates)),
        ],
        compiler_params=pltpu.CompilerParams(
            collective_id=0, has_side_effects=True, vmem_limit_bytes=64 * 1024 * 1024 - 65536
        ),
    )(points, exemplars, selection.reshape(levels, tall, LANES))
    gains, cover = pl.pallas_call(
        hand_out,
        out_shape=tuple(jax.ShapeDtypeStruct(x.shape, x.dtype) for x in (gains, cover)),
        in_specs=[vmem] * 2,
        out_specs=(vmem, vmem),
    )(gains, cover)
    return gains.reshape(levels, 1, 2 * width), cover.reshape(count)


def solution(mesh):
    placed = (
        P(("parts", "leaf", "inner", "sub"), None),
        P(("parts", "leaf"), None, None),
        P(None, ("parts", "leaf"), None),
    )
    return jax.shard_map(
        on_device,
        mesh=mesh,
        in_specs=placed,
        out_specs=(P(None, ("parts", "leaf"), None), P(("parts", "leaf", "inner", "sub"))),
        check_vma=False,
    )
```
